32 devices in a mesh: band: 4 (over z), owner: 8 (over y, x, core).
Axes of the slice: x: 2, y: 2, z: 4, core: 2. Of those that a mesh axis runs over, the one named last changes fastest.
Arguments:
- user_factors: float32 [16384, 256], P(('band', 'owner')), may hold values from -1.5 to 1.5
- item_factors: float32 [4096, 256], P(('band', 'owner')), may hold values from -1.5 to 1.5
- ratings: bfloat16 [3, 512, 128, 128], P(None, ('band', 'owner')), may hold values from -6 to 6
- tile_users: int32 [3, 512], P(None, ('band', 'owner')), may hold values from 0 to 3, as said below
- tile_items: int32 [3, 512], P(None, ('band', 'owner')), may hold values from 0 to 7, as said below
- tile_count: int32 [3, 32], P(None, ('band', 'owner')), may hold values from 1 to 16, as said below
Outputs:
- user_out: float32 [16384, 256], P(('band', 'owner'))
- item_out: float32 [4096, 256], P(('band', 'owner'))
The draws below stay inside these ranges and needn't reach their ends.
Inputs may be any that keep to these rules, and one draw needn't show every extreme that they name: `tile_users`: within one device and tick, the slots name distinct tiles (user row, item column). `tile_items`: paired with tile_users: the slots of one device and tick name distinct tiles. `tile_count`: each value is 16, 8 or 4, at least 1; in every tick some device has 16.
All inputs are finite; a program needn't handle non-finite values.
Results may differ from the reference program's by a relative error of at most 0.0003.
Values sent between devices are 32-bit elements; how exact they have to be, the bound alone decides.
A program may use at most 64 MiB of HBM per device.

```python
import jax
import jax.numpy as jnp
from jax import lax

R = 256
P_SIZE = 1024
TILE = 128
TICKS = 3
U_DEV = 512
K_MAX = 16
USERS = 16384
ITEMS = 4096
SLOTS = 512
N_BAND = 4
N_OWNER = 8


def tile_cells(key):
    base = jax.random.fold_in(key, 7)
    cells = U_DEV // TILE * (P_SIZE // TILE)
    groups = SLOTS // K_MAX
    subkeys = jax.random.split(base, TICKS * groups)

    def pick_cells(subkey):
        return jax.random.permutation(subkey, cells)[:K_MAX]
    chosen = jax.vmap(pick_cells)(subkeys)
    return chosen.reshape(TICKS, SLOTS).astype(jnp.int32)


def draw_tile_users(key, part):
    return (tile_cells(key) // (P_SIZE // TILE)).astype(jnp.int32)


def draw_tile_items(key, part):
    return (tile_cells(key) % (P_SIZE // TILE)).astype(jnp.int32)


def draw_tile_count(key, part):
    groups = SLOTS // K_MAX
    first_key, second_key = jax.random.split(jax.random.fold_in(key, 11))
    powers = jax.random.randint(first_key, (TICKS, groups), 0, 3)
    filled = jnp.where(powers == 0, K_MAX, jnp.where(powers == 1, K_MAX // 2, K_MAX // 4))
    filled = jnp.maximum(filled, 1)
    places = jax.random.randint(second_key, (TICKS,), 0, groups)
    filled = filled.at[jnp.arange(TICKS), places].set(K_MAX)
    return filled.astype(jnp.int32)


def steps_of(key, dims, shards, least, high):
    gain, own = 1.0, jax.random.fold_in(key, 6)
    for axis_at, shards_of in shards:
        steps = jnp.exp(jax.random.uniform(jax.random.fold_in(own, axis_at), (shards_of,), jnp.float32, least / len(shards), high / len(shards)))
        gain = gain * jnp.repeat(steps, dims[axis_at] // shards_of).reshape([-1 if axis == axis_at else 1 for axis in range(len(dims))])
    return gain


def scatter_about(own_key, extent, width, bound, pieces=(), kind=jnp.bfloat16):
    drawn = width * jax.random.normal(own_key, extent, jnp.float32)
    if pieces:
        drawn = drawn * steps_of(own_key, extent, pieces, -0.22, 0.18)
    return jnp.clip(drawn, -bound, bound).astype(kind)


def setup_inputs(seed: int = 0) -> dict:
    keys = jax.random.split(jax.random.key(seed), 7)
    user_factors = scatter_about(keys[0], (USERS, R), 0.25, 1.5, ((0, 32),), jnp.float32)
    item_factors = scatter_about(keys[1], (ITEMS, R), 0.25, 1.5, ((0, 32),), jnp.float32)
    ratings = scatter_about(keys[2], (TICKS, SLOTS, TILE, TILE), 1.0, 6.0, ((1, 32),))
    tile_users = draw_tile_users(jax.random.fold_in(keys[6], 71), 0)
    tile_items = draw_tile_items(jax.random.fold_in(keys[6], 71), 0)
    tile_count = draw_tile_count(jax.random.fold_in(keys[6], 71), 0)
    return dict(user_factors=user_factors, item_factors=item_factors, ratings=ratings, tile_users=tile_users, tile_items=tile_items, tile_count=tile_count)


user_rate = 0.02
item_rate = 0.005
shrink_rate = 0.05
highest = lax.Precision.HIGHEST


def slot_update(user_block, item_panel, rating_tiles, tile_rows, tile_cols, filled):
    user_tiles = user_block[tile_rows]
    item_tiles = item_panel[tile_cols]
    active = (jnp.arange(K_MAX) < filled).astype(jnp.float32)
    predicted = jnp.einsum("kur,kir->kui", user_tiles, item_tiles, precision=highest)
    errors = (rating_tiles.astype(jnp.float32) - predicted) * active[:, None, None]
    user_grads = jnp.einsum("kui,kir->kur", errors, item_tiles, precision=highest)
    item_grads = jnp.einsum("kui,kur->kir", errors, user_tiles, precision=highest)
    user_hot = (tile_rows[:, None] == jnp.arange(user_block.shape[0])[None, :]).astype(jnp.float32)
    item_hot = (tile_cols[:, None] == jnp.arange(item_panel.shape[0])[None, :]).astype(jnp.float32)
    user_sum = jnp.einsum("kt,kur->tur", user_hot, user_grads, precision=highest)
    item_sum = jnp.einsum("kt,kir->tir", item_hot, item_grads, precision=highest)
    new_users = user_block * (1.0 - user_rate * shrink_rate) + user_rate * user_sum
    return new_users, item_sum


def reference(user_factors, item_factors, ratings, tile_users, tile_items, tile_count):
    bands = N_BAND
    owners = N_OWNER
    user_blocks = user_factors.reshape(bands, owners, U_DEV // TILE, TILE, R)
    panels_all = item_factors.reshape(bands, P_SIZE // TILE, TILE, R)
    for tick_index in range(TICKS):
        rating_tiles = ratings[tick_index].reshape(bands, owners, K_MAX, TILE, TILE)
        tile_rows = tile_users[tick_index].reshape(bands, owners, K_MAX)
        tile_cols = tile_items[tick_index].reshape(bands, owners, K_MAX)
        filled = tile_count[tick_index].reshape(bands, owners)
        current = jnp.roll(panels_all, -tick_index, axis=0)

        def band_step(operands):
            block, item_panel, tiles_here, rows_here, cols_here, filled_here = operands
            new_users, item_sums = jax.vmap(slot_update, in_axes=(0, None, 0, 0, 0, 0))(
                block, item_panel, tiles_here, rows_here, cols_here, filled_here)
            new_panel = item_panel * (1.0 - item_rate * shrink_rate) + item_rate * jnp.sum(item_sums, axis=0)
            return new_users, new_panel

        user_blocks, current = lax.map(band_step, (user_blocks, current, rating_tiles, tile_rows, tile_cols, filled))
        panels_all = jnp.roll(current, tick_index, axis=0)
    final_panels = jnp.roll(panels_all, -(TICKS - 1), axis=0)
    return user_blocks.reshape(-1, R), final_panels.reshape(-1, R)
```

```python
import functools

import jax
import jax.numpy as jnp
from jax import lax
from jax.experimental import pallas as pl
from jax.experimental.pallas import tpu as pltpu
from jax.sharding import PartitionSpec as P

user_rate = 0.02
item_rate = 0.005
shrink_rate = 0.05
MESH = pl.DeviceIdType.MESH
f32 = jnp.float32
bf16 = jnp.bfloat16


def halves(x):
    high = x.astype(bf16)
    return high, (x - high.astype(f32)).astype(bf16)


def dot3(a, b, dims):
    (ah, al), (bh, bl) = a, b

    def one(x, y):
        return lax.dot_general(x, y, (dims, ((), ())), preferred_element_type=f32)

    return one(ah, bh) + (one(ah, bl) + one(al, bh))


def kernel(cfg, slot_ref, live_ref, users_ref, items_ref, ratings_ref, users_out, items_out,
           panel, from_sibling, from_chips, partial, combined, grad, uh, ul, eh, el,
           fresh, ag_send, ag_recv, fwd_send, fwd_recv, ps_send, ps_recv, rs_send, rs_recv,
           pm_send, pm_recv):
    ticks, bands, chips, share, group, tile, user_tiles, item_tiles = cfg
    groups = chips // group
    wide = 2 * share * group
    band = lax.axis_index("band")
    owner = lax.axis_index("owner")
    chip, core = owner // 2, owner % 2
    mine, within = chip // group, chip % group
    sibling = (band, chip * 2 + 1 - core)

    def group_at(s):
        if groups % 2:
            return (mine + s) % groups
        return ((mine // 2 + s // 2) % (groups // 2)) * 2 + (mine % 2 + s % 2) % 2

    def chip_at(s, j):
        return group_at(s) * group + (within + j) % group

    def own(s, j):
        return s == 0 and j == 0

    def rows(c, k):
        return pl.ds(pl.multiple_of((c * 2 + k) * share, share), share)

    def within_block(s, c, k):
        return pl.ds(pl.multiple_of(((c % group) * 2 + k) * share, share), share)

    def to(c):
        return (band, c * 2 + core)

    pairs = [(s, j) for s in range(groups) for j in range(group)]
    others = [p for p in pairs if not own(*p)]
    back = ((band + bands - 1) % bands, owner)
    ahead = ((band + 1) % bands, owner)

    barrier = pltpu.get_barrier_semaphore()
    for device in [sibling, back, ahead] + [to(chip_at(*p)) for p in others]:
        pl.semaphore_signal(barrier, inc=1, device_id=device, device_id_type=MESH)
    pl.semaphore_wait(barrier, 3 + len(others))

    def remote(src, dst, ssem, rsem, device):
        return pltpu.make_async_remote_copy(
            src_ref=src, dst_ref=dst, send_sem=ssem, recv_sem=rsem,
            device_id=device, device_id_type=MESH)

    users_out[...] = users_ref[...]
    panel[0, rows(chip, core), :] = items_ref[...]

    def tick(t, carry):
        def gather(s, j):
            here = panel.at[t, rows(chip, core), :]
            c = chip_at(s, j)
            return remote(here, here, ag_send.at[t, c], ag_recv.at[t, chip], to(c))

        def gathered(s, j):
            c = chip_at(s, j)
            here = panel.at[t, rows(c, core), :]
            return remote(here, here, ag_send.at[t, c], ag_recv.at[t, c], to(c))

        def forward(s, j):
            c = chip_at(s, j)
            here = panel.at[t, rows(c, core), :]
            return remote(here, here, fwd_send.at[t, c], fwd_recv.at[t, c], sibling)

        def forwarded(s, j):
            c = chip_at(s, j)
            here = panel.at[t, rows(c, 1 - core), :]
            return remote(here, here, fwd_send.at[t, c], fwd_recv.at[t, c], sibling)

        def hand_over(s, j):
            c = chip_at(s, j)
            return remote(partial.at[s, within_block(s, c, 1 - core), :], from_sibling.at[t, c],
                          ps_send.at[t, c], ps_recv.at[t, c], sibling)

        def scatter(s, j):
            c = chip_at(s, j)
            return remote(combined.at[c], from_chips.at[t, chip],
                          rs_send.at[t, c], rs_recv.at[t, chip], to(c))

        def scattered(s, j):
            c = chip_at(s, j)
            return remote(combined.at[c], from_chips.at[t, c],
                          rs_send.at[t, c], rs_recv.at[t, c], to(c))

        def pass_back(here, there):
            return remote(fresh.at[here], panel.at[there, rows(chip, core), :],
                          pm_send.at[here], pm_recv.at[there], back)

        @pl.when(t > 0)
        def _():
            pass_back(t - 1, t).wait_recv()

        for p in others:
            gather(*p).start()
        forward(0, 0).start()

        high, low = halves(users_out[...])
        uh[...] = high
        ul[...] = low

        def block(s):
            g = group_at(s)
            v = halves(panel[t, pl.ds(pl.multiple_of(g * wide, wide), wide), :])
            for i in range(user_tiles):
                here = pl.ds(i * tile, tile)
                pred = dot3((uh[here, :], ul[here, :]), v, ((1,), (1,)))
                parts = []
                for j in range(wide // tile):
                    cell = i * item_tiles + g * (wide // tile) + j
                    rating = ratings_ref[t, slot_ref[t, cell]].astype(f32)
                    parts.append((rating - pred[:, j * tile:(j + 1) * tile]) * live_ref[t, cell])
                e = halves(jnp.concatenate(parts, axis=1))
                eh[here, :] = e[0]
                el[here, :] = e[1]
                step = dot3(e, v, ((1,), (0,)))
                if s == 0:
                    grad[here, :] = step
                else:
                    grad[here, :] += step
            partial[s] = dot3((eh[...], el[...]), (uh[...], ul[...]), ((0,), (0,)))

        def combine(s):
            for j in range(group):
                c = chip_at(s, j)
                hand_over(s, j).wait_recv()
                combined[c] = partial[s, within_block(s, c, core), :] + from_sibling[t, c]
                if not own(s, j):
                    scatter(s, j).start()

        for s in range(groups):
            for j in range(group):
                if not own(s, j):
                    gathered(s, j).wait_recv()
                    forward(s, j).start()
            if s:
                combine(s - 1)
            for j in range(group):
                forwarded(s, j).wait_recv()
            block(s)
            for j in range(group):
                hand_over(s, j).start()
        users_out[...] = users_out[...] * (1.0 - user_rate * shrink_rate) + user_rate * grad[...]
        combine(groups - 1)

        total = combined[chip]
        for p in others:
            scattered(*p).wait_recv()
            total = total + from_chips[t, chip_at(*p)]
        new = panel[t, rows(chip, core), :] * (1.0 - item_rate * shrink_rate) + item_rate * total

        @pl.when(t < ticks - 1)
        def _():
            fresh[t] = new
            pass_back(t, t + 1).start()

        @pl.when(t == ticks - 1)
        def _():
            items_out[...] = new

        for p in pairs:
            forward(*p).wait_send()
            hand_over(*p).wait_send()
            if not own(*p):
                gather(*p).wait_send()
                scatter(*p).wait_send()

        @pl.when(t > 0)
        def _():
            pass_back(t - 1, t).wait_send()

        return carry

    lax.fori_loop(0, ticks, tick, 0)


def shards(bands, owners, user_factors, item_factors, ratings, tile_users, tile_items, tile_count):
    ticks, slots, tile, _ = ratings.shape
    users, rank = user_factors.shape
    share = item_factors.shape[0]
    chips = owners // 2
    panel_rows = share * owners
    user_tiles, item_tiles = users // tile, panel_rows // tile
    group = max(1, 2 * tile // (2 * share))
    groups, wide = chips // group, 2 * share * group

    number = jnp.arange(slots, dtype=jnp.int32)[None, :]
    cell = jnp.where(number < tile_count, tile_users * item_tiles + tile_items, -1)
    hit = cell[:, :, None] == jnp.arange(user_tiles * item_tiles, dtype=jnp.int32)[None, None, :]
    slot_of = jnp.sum(jnp.where(hit, number[:, :, None], 0), axis=1)
    live = jnp.sum(hit.astype(f32), axis=1)

    cfg = (ticks, bands, chips, share, group, tile, user_tiles, item_tiles)
    vmem = pl.BlockSpec(memory_space=pltpu.VMEM)
    smem = pl.BlockSpec(memory_space=pltpu.SMEM)
    sems = pltpu.SemaphoreType.DMA((ticks, chips))
    work = 18 * ticks * users * panel_rows * rank
    return pl.pallas_call(
        functools.partial(kernel, cfg),
        out_shape=(jax.ShapeDtypeStruct((users, rank), f32), jax.ShapeDtypeStruct((share, rank), f32)),
        in_specs=[smem, smem, vmem, vmem, vmem],
        out_specs=(vmem, vmem),
        scratch_shapes=[
            pltpu.VMEM((ticks, panel_rows, rank), f32),
            pltpu.VMEM((ticks, chips, share, rank), f32),
            pltpu.VMEM((ticks, chips, share, rank), f32),
            pltpu.VMEM((groups, wide, rank), f32),
            pltpu.VMEM((chips, share, rank), f32),
            pltpu.VMEM((users, rank), f32),
            pltpu.VMEM((users, rank), bf16),
            pltpu.VMEM((users, rank), bf16),
            pltpu.VMEM((users, wide), bf16),
            pltpu.VMEM((users, wide), bf16),
            pltpu.VMEM((ticks, share, rank), f32),
        ] + [sems] * 8 + [pltpu.SemaphoreType.DMA((ticks,))] * 2,
        compiler_params=pltpu.CompilerParams(
            collective_id=0, has_side_effects=True, vmem_limit_bytes=48 * 1024 * 1024),
        cost_estimate=pl.CostEstimate(flops=work, bytes_accessed=8 * 1024 * 1024, transcendentals=0),
    )(slot_of, live, user_factors, item_factors, ratings)


def solution(mesh):
    both = ("band", "owner")
    placed = (P(both, None), P(both, None), P(None, both, None, None), P(None, both), P(None, both), P(None, both))
    return jax.shard_map(
        functools.partial(shards, mesh.shape["band"], mesh.shape["owner"]),
        mesh=mesh,
        in_specs=placed,
        out_specs=(P(both, None), P(both, None)),
        check_vma=False,
    )
```

```python
import functools

import jax
import jax.numpy as jnp
from jax import lax
from jax.experimental import pallas as pl
from jax.experimental.pallas import tpu as pltpu
from jax.sharding import PartitionSpec as P

user_rate = 0.02
item_rate = 0.005
shrink_rate = 0.05
MESH = pl.DeviceIdType.MESH
f32 = jnp.float32
bf16 = jnp.bfloat16


def halves(x):
    high = x.astype(bf16)
    return high, (x - high.astype(f32)).astype(bf16)


def dot3(a, b, dims):
    (ah, al), (bh, bl) = a, b

    def one(x, y):
        return lax.dot_general(x, y, (dims, ((), ())), preferred_element_type=f32)

    return one(ah, bh) + (one(ah, bl) + one(al, bh))


def kernel(cfg, slot_ref, live_ref, users_ref, items_ref, ratings_hbm, users_out, items_out,
           panel, from_sibling, from_chips, partial, combined, grad, uh, ul, eh, el,
           fresh, ag_send, ag_recv, fwd_send, fwd_recv, ps_send, ps_recv, rs_send, rs_recv,
           pm_send, pm_recv, ratings_ref, load_sem):
    ticks, bands, chips, share, group, tile, user_tiles, item_tiles = cfg
    groups = chips // group
    wide = 2 * share * group
    band = lax.axis_index("band")
    owner = lax.axis_index("owner")
    chip, core = owner // 2, owner % 2
    mine, within = chip // group, chip % group
    sibling = (band, chip * 2 + 1 - core)

    def group_at(s):
        s = (groups - s) % groups
        if groups % 2:
            return (mine + s) % groups
        return ((mine // 2 + s // 2) % (groups // 2)) * 2 + (mine % 2 + s % 2) % 2

    def chip_at(s, j):
        return group_at(s) * group + (within + j) % group

    def own(s, j):
        return s == 0 and j == 0

    def rows(c, k):
        return pl.ds(pl.multiple_of((c * 2 + k) * share, share), share)

    def within_block(s, c, k):
        return pl.ds(pl.multiple_of(((c % group) * 2 + k) * share, share), share)

    def to(c):
        return (band, c * 2 + core)

    pairs = [(s, j) for s in range(groups) for j in range(group)]
    others = [p for p in pairs if not own(*p)]
    back = ((band + bands - 1) % bands, owner)
    ahead = ((band + 1) % bands, owner)

    load_users = pltpu.make_async_copy(users_ref, users_out, load_sem.at[0])
    load_ratings = pltpu.make_async_copy(ratings_hbm, ratings_ref, load_sem.at[1])
    load_users.start()
    load_ratings.start()

    barrier = pltpu.get_barrier_semaphore()
    for device in [sibling, back, ahead] + [to(chip_at(*p)) for p in others]:
        pl.semaphore_signal(barrier, inc=1, device_id=device, device_id_type=MESH)
    pl.semaphore_wait(barrier, 3 + len(others))

    def remote(src, dst, ssem, rsem, device):
        return pltpu.make_async_remote_copy(
            src_ref=src, dst_ref=dst, send_sem=ssem, recv_sem=rsem,
            device_id=device, device_id_type=MESH)

    panel[0, rows(chip, core), :] = items_ref[...]

    def tick(t, carry):
        def gather(s, j):
            here = panel.at[t, rows(chip, core), :]
            c = chip_at(s, j)
            return remote(here, here, ag_send.at[t, c], ag_recv.at[t, chip], to(c))

        def gathered(s, j):
            c = chip_at(s, j)
            here = panel.at[t, rows(c, core), :]
            return remote(here, here, ag_send.at[t, c], ag_recv.at[t, c], to(c))

        def forward(s, j):
            c = chip_at(s, j)
            here = panel.at[t, rows(c, core), :]
            return remote(here, here, fwd_send.at[t, c], fwd_recv.at[t, c], sibling)

        def forwarded(s, j):
            c = chip_at(s, j)
            here = panel.at[t, rows(c, 1 - core), :]
            return remote(here, here, fwd_send.at[t, c], fwd_recv.at[t, c], sibling)

        def hand_over(s, j):
            c = chip_at(s, j)
            return remote(partial.at[s, within_block(s, c, 1 - core), :], from_sibling.at[t, c],
                          ps_send.at[t, c], ps_recv.at[t, c], sibling)

        def scatter(s, j):
            c = chip_at(s, j)
            return remote(combined.at[c], from_chips.at[t, chip],
                          rs_send.at[t, c], rs_recv.at[t, chip], to(c))

        def scattered(s, j):
            c = chip_at(s, j)
            return remote(combined.at[c], from_chips.at[t, c],
                          rs_send.at[t, c], rs_recv.at[t, c], to(c))

        def pass_back(here, there):
            return remote(fresh.at[here], panel.at[there, rows(chip, core), :],
                          pm_send.at[here], pm_recv.at[there], back)

        @pl.when(t > 0)
        def _():
            pass_back(t - 1, t).wait_recv()

        for p in others:
            gather(*p).start()
        forward(0, 0).start()

        @pl.when(t == 0)
        def _():
            load_users.wait()
            load_ratings.wait()

        high, low = halves(users_out[...])
        uh[...] = high
        ul[...] = low

        def block(s):
            g = group_at(s)
            v = halves(panel[t, pl.ds(pl.multiple_of(g * wide, wide), wide), :])
            for i in range(user_tiles):
                here = pl.ds(i * tile, tile)
                pred = dot3((uh[here, :], ul[here, :]), v, ((1,), (1,)))
                parts = []
                for j in range(wide // tile):
                    cell = i * item_tiles + g * (wide // tile) + j
                    rating = ratings_ref[t, slot_ref[t, cell]].astype(f32)
                    parts.append((rating - pred[:, j * tile:(j + 1) * tile]) * live_ref[t, cell])
                e = halves(jnp.concatenate(parts, axis=1))
                eh[here, :] = e[0]
                el[here, :] = e[1]
                step = dot3(e, v, ((1,), (0,)))
                if s == 0:
                    grad[here, :] = step
                else:
                    grad[here, :] += step
            partial[s] = dot3((eh[...], el[...]), (uh[...], ul[...]), ((0,), (0,)))

        def combine(s):
            for j in range(group):
                c = chip_at(s, j)
                hand_over(s, j).wait_recv()
                combined[c] = partial[s, within_block(s, c, core), :] + from_sibling[t, c]
                if not own(s, j):
                    scatter(s, j).start()

        def receive(s):
            for j in range(group):
                if not own(s, j):
                    gathered(s, j).wait_recv()
                    forward(s, j).start()

        for s in range(groups):
            receive(s)
            if s:
                combine(s - 1)
            for j in range(group):
                forwarded(s, j).wait_recv()
            block(s)
            for j in range(group):
                hand_over(s, j).start()
        users_out[...] = users_out[...] * (1.0 - user_rate * shrink_rate) + user_rate * grad[...]
        combine(groups - 1)

        total = combined[chip]
        for p in others:
            scattered(*p).wait_recv()
            total = total + from_chips[t, chip_at(*p)]
        new = panel[t, rows(chip, core), :] * (1.0 - item_rate * shrink_rate) + item_rate * total

        @pl.when(t < ticks - 1)
        def _():
            fresh[t] = new
            pass_back(t, t + 1).start()

        @pl.when(t == ticks - 1)
        def _():
            items_out[...] = new

        for p in pairs:
            forward(*p).wait_send()
            hand_over(*p).wait_send()
            if not own(*p):
                gather(*p).wait_send()
                scatter(*p).wait_send()

        @pl.when(t > 0)
        def _():
            pass_back(t - 1, t).wait_send()

        return carry

    lax.fori_loop(0, ticks, tick, 0)


def shards(bands, owners, user_factors, item_factors, ratings, tile_users, tile_items, tile_count):
    ticks, slots, tile, _ = ratings.shape
    users, rank = user_factors.shape
    share = item_factors.shape[0]
    chips = owners // 2
    panel_rows = share * owners
    user_tiles, item_tiles = users // tile, panel_rows // tile
    group = max(1, 2 * tile // (2 * share))
    groups, wide = chips // group, 2 * share * group

    number = jnp.arange(slots, dtype=jnp.int32)[None, :]
    cell = jnp.where(number < tile_count, tile_users * item_tiles + tile_items, -1)
    hit = cell[:, :, None] == jnp.arange(user_tiles * item_tiles, dtype=jnp.int32)[None, None, :]
    slot_of = jnp.sum(jnp.where(hit, number[:, :, None], 0), axis=1)
    live = jnp.sum(hit.astype(f32), axis=1)

    cfg = (ticks, bands, chips, share, group, tile, user_tiles, item_tiles)
    vmem = pl.BlockSpec(memory_space=pltpu.VMEM)
    hbm = pl.BlockSpec(memory_space=pltpu.HBM)
    smem = pl.BlockSpec(memory_space=pltpu.SMEM)
    sems = pltpu.SemaphoreType.DMA((ticks, chips))
    work = 18 * ticks * users * panel_rows * rank
    return pl.pallas_call(
        functools.partial(kernel, cfg),
        out_shape=(jax.ShapeDtypeStruct((users, rank), f32), jax.ShapeDtypeStruct((share, rank), f32)),
        in_specs=[smem, smem, hbm, vmem, hbm],
        out_specs=(vmem, vmem),
        scratch_shapes=[
            pltpu.VMEM((ticks, panel_rows, rank), f32),
            pltpu.VMEM((ticks, chips, share, rank), f32),
            pltpu.VMEM((ticks, chips, share, rank), f32),
            pltpu.VMEM((groups, wide, rank), f32),
            pltpu.VMEM((chips, share, rank), f32),
            pltpu.VMEM((users, rank), f32),
            pltpu.VMEM((users, rank), bf16),
            pltpu.VMEM((users, rank), bf16),
            pltpu.VMEM((users, wide), bf16),
            pltpu.VMEM((users, wide), bf16),
            pltpu.VMEM((ticks, share, rank), f32),
        ] + [sems] * 8 + [pltpu.SemaphoreType.DMA((ticks,))] * 2 + [
            pltpu.VMEM(ratings.shape, ratings.dtype), pltpu.SemaphoreType.DMA((2,))],
        compiler_params=pltpu.CompilerParams(
            collective_id=0, has_side_effects=True, vmem_limit_bytes=48 * 1024 * 1024),
        cost_estimate=pl.CostEstimate(flops=work, bytes_accessed=8 * 1024 * 1024, transcendentals=0),
    )(slot_of, live, user_factors, item_factors, ratings)


def solution(mesh):
    both = ("band", "owner")
    placed = (P(both, None), P(both, None), P(None, both, None, None), P(None, both), P(None, both), P(None, both))
    return jax.shard_map(
        functools.partial(shards, mesh.shape["band"], mesh.shape["owner"]),
        mesh=mesh,
        in_specs=placed,
        out_specs=(P(both, None), P(both, None)),
        check_vma=False,
    )
```

```python
import functools

import jax
import jax.numpy as jnp
from jax import lax
from jax.experimental import pallas as pl
from jax.experimental.pallas import tpu as pltpu
from jax.sharding import PartitionSpec as P

user_rate = 0.02
item_rate = 0.005
shrink_rate = 0.05
MESH = pl.DeviceIdType.MESH
f32 = jnp.float32
bf16 = jnp.bfloat16


def halves(x):
    high = x.astype(bf16)
    return high, (x - high.astype(f32)).astype(bf16)


def dot3(a, b, dims):
    (ah, al), (bh, bl) = a, b

    def one(x, y):
        return lax.dot_general(x, y, (dims, ((), ())), preferred_element_type=f32)

    return one(ah, bh) + (one(ah, bl) + one(al, bh))


def kernel(cfg, slot_ref, live_ref, users_ref, items_ref, ratings_hbm, users_out, items_out,
           panel, from_sibling, from_chips, partial, combined, grad, uh, ul, eh, el,
           vh, vl, fresh, ag_send, ag_recv, fwd_send, fwd_recv, ps_send, ps_recv, rs_send, rs_recv,
           pm_send, pm_recv, ratings_ref, load_sem):
    ticks, bands, chips, share, group, tile, user_tiles, item_tiles = cfg
    groups = chips // group
    wide = 2 * share * group
    band = lax.axis_index("band")
    owner = lax.axis_index("owner")
    chip, core = owner // 2, owner % 2
    mine, within = chip // group, chip % group
    sibling = (band, chip * 2 + 1 - core)

    def group_at(s):
        s = (groups - s) % groups
        if groups % 2:
            return (mine + s) % groups
        return ((mine // 2 + s // 2) % (groups // 2)) * 2 + (mine % 2 + s % 2) % 2

    def chip_at(s, j):
        return group_at(s) * group + (within + j) % group

    def own(s, j):
        return s == 0 and j == 0

    def rows(c, k):
        return pl.ds(pl.multiple_of((c * 2 + k) * share, share), share)

    def within_block(s, c, k):
        return pl.ds(pl.multiple_of(((c % group) * 2 + k) * share, share), share)

    def to(c):
        return (band, c * 2 + core)

    pairs = [(s, j) for s in range(groups) for j in range(group)]
    others = [p for p in pairs if not own(*p)]
    back = ((band + bands - 1) % bands, owner)
    ahead = ((band + 1) % bands, owner)

    load_users = pltpu.make_async_copy(users_ref, users_out, load_sem.at[0])
    load_ratings = pltpu.make_async_copy(ratings_hbm, ratings_ref, load_sem.at[1])
    load_users.start()
    load_ratings.start()

    barrier = pltpu.get_barrier_semaphore()
    for device in [sibling, back, ahead] + [to(chip_at(*p)) for p in others]:
        pl.semaphore_signal(barrier, inc=1, device_id=device, device_id_type=MESH)
    pl.semaphore_wait(barrier, 3 + len(others))

    def remote(src, dst, ssem, rsem, device):
        return pltpu.make_async_remote_copy(
            src_ref=src, dst_ref=dst, send_sem=ssem, recv_sem=rsem,
            device_id=device, device_id_type=MESH)

    panel[0, rows(chip, core), :] = items_ref[...]

    def tick(t, carry):
        def gather(s, j):
            here = panel.at[t, rows(chip, core), :]
            c = chip_at(s, j)
            return remote(here, here, ag_send.at[t, c], ag_recv.at[t, chip], to(c))

        def gathered(s, j):
            c = chip_at(s, j)
            here = panel.at[t, rows(c, core), :]
            return remote(here, here, ag_send.at[t, c], ag_recv.at[t, c], to(c))

        def forward(s, j):
            c = chip_at(s, j)
            here = panel.at[t, rows(c, core), :]
            return remote(here, here, fwd_send.at[t, c], fwd_recv.at[t, c], sibling)

        def forwarded(s, j):
            c = chip_at(s, j)
            here = panel.at[t, rows(c, 1 - core), :]
            return remote(here, here, fwd_send.at[t, c], fwd_recv.at[t, c], sibling)

        def hand_over(s, j):
            c = chip_at(s, j)
            return remote(partial.at[s, within_block(s, c, 1 - core), :], from_sibling.at[t, c],
                          ps_send.at[t, c], ps_recv.at[t, c], sibling)

        def scatter(s, j):
            c = chip_at(s, j)
            return remote(combined.at[c], from_chips.at[t, chip],
                          rs_send.at[t, c], rs_recv.at[t, chip], to(c))

        def scattered(s, j):
            c = chip_at(s, j)
            return remote(combined.at[c], from_chips.at[t, c],
                          rs_send.at[t, c], rs_recv.at[t, c], to(c))

        def pass_back(here, there):
            return remote(fresh.at[here], panel.at[there, rows(chip, core), :],
                          pm_send.at[here], pm_recv.at[there], back)

        @pl.when(t > 0)
        def _():
            pass_back(t - 1, t).wait_recv()

        for p in others:
            gather(*p).start()
        forward(0, 0).start()

        @pl.when(t == 0)
        def _():
            load_users.wait()
            load_ratings.wait()

        high, low = halves(users_out[...])
        uh[...] = high
        ul[...] = low

        def block(s):
            g = group_at(s)
            v = halves(panel[t, pl.ds(pl.multiple_of(g * wide, wide), wide), :])
            vh[s] = v[0]
            vl[s] = v[1]
            for i in range(user_tiles):
                here = pl.ds(i * tile, tile)
                pred = dot3((uh[here, :], ul[here, :]), v, ((1,), (1,)))
                parts = []
                for j in range(wide // tile):
                    cell = i * item_tiles + g * (wide // tile) + j
                    rating = ratings_ref[t, slot_ref[t, cell]].astype(f32)
                    parts.append((rating - pred[:, j * tile:(j + 1) * tile]) * live_ref[t, cell])
                high, low = halves(jnp.concatenate(parts, axis=1))
                eh[s, here, :] = high
                el[s, here, :] = low
            u = (uh[...], ul[...])
            if group == 1 and share % tile == 0:
                for k in (1 - core, core):
                    part = pl.ds(pl.multiple_of(k * share, share), share)
                    partial[s, part, :] = dot3((eh[s, :, part], el[s, :, part]), u, ((0,), (0,)))
                    if k is not core:
                        hand_over(s, 0).start()
            else:
                partial[s] = dot3((eh[s], el[s]), u, ((0,), (0,)))
                for j in range(group):
                    hand_over(s, j).start()

        def user_step(s):
            for i in range(user_tiles):
                here = pl.ds(i * tile, tile)
                step = dot3((eh[s, here, :], el[s, here, :]), (vh[s], vl[s]), ((1,), (0,)))
                if s == 0:
                    grad[here, :] = step
                else:
                    grad[here, :] += step

        def combine(s):
            for j in range(group):
                c = chip_at(s, j)
                hand_over(s, j).wait_recv()
                combined[c] = partial[s, within_block(s, c, core), :] + from_sibling[t, c]
                if not own(s, j):
                    scatter(s, j).start()

        def receive(s):
            for j in range(group):
                if not own(s, j):
                    gathered(s, j).wait_recv()
                    forward(s, j).start()

        for s in range(groups):
            receive(s)
            if s:
                combine(s - 1)
            for j in range(group):
                forwarded(s, j).wait_recv()
            block(s)
        combine(groups - 1)
        early = groups - 0
        for s in range(early):
            user_step(s)

        total = combined[chip]
        for p in others:
            scattered(*p).wait_recv()
            total = total + from_chips[t, chip_at(*p)]
        new = panel[t, rows(chip, core), :] * (1.0 - item_rate * shrink_rate) + item_rate * total

        @pl.when(t < ticks - 1)
        def _():
            fresh[t] = new
            pass_back(t, t + 1).start()

        @pl.when(t == ticks - 1)
        def _():
            items_out[...] = new

        for s in range(early, groups):
            user_step(s)
        users_out[...] = users_out[...] * (1.0 - user_rate * shrink_rate) + user_rate * grad[...]

        for p in pairs:
            forward(*p).wait_send()
            hand_over(*p).wait_send()
            if not own(*p):
                gather(*p).wait_send()
                scatter(*p).wait_send()

        @pl.when(t > 0)
        def _():
            pass_back(t - 1, t).wait_send()

        return carry

    lax.fori_loop(0, ticks, tick, 0)


def shards(bands, owners, user_factors, item_factors, ratings, tile_users, tile_items, tile_count):
    ticks, slots, tile, _ = ratings.shape
    users, rank = user_factors.shape
    share = item_factors.shape[0]
    chips = owners // 2
    panel_rows = share * owners
    user_tiles, item_tiles = users // tile, panel_rows // tile
    group = max(1, 2 * tile // (2 * share))
    groups, wide = chips // group, 2 * share * group

    number = jnp.arange(slots, dtype=jnp.int32)[None, :]
    cell = jnp.where(number < tile_count, tile_users * item_tiles + tile_items, -1)
    hit = cell[:, :, None] == jnp.arange(user_tiles * item_tiles, dtype=jnp.int32)[None, None, :]
    slot_of = jnp.sum(jnp.where(hit, number[:, :, None], 0), axis=1)
    live = jnp.sum(hit.astype(f32), axis=1)

    cfg = (ticks, bands, chips, share, group, tile, user_tiles, item_tiles)
    vmem = pl.BlockSpec(memory_space=pltpu.VMEM)
    hbm = pl.BlockSpec(memory_space=pltpu.HBM)
    smem = pl.BlockSpec(memory_space=pltpu.SMEM)
    sems = pltpu.SemaphoreType.DMA((ticks, chips))
    work = 18 * ticks * users * panel_rows * rank
    return pl.pallas_call(
        functools.partial(kernel, cfg),
        out_shape=(jax.ShapeDtypeStruct((users, rank), f32), jax.ShapeDtypeStruct((share, rank), f32)),
        in_specs=[smem, smem, hbm, vmem, hbm],
        out_specs=(vmem, vmem),
        scratch_shapes=[
            pltpu.VMEM((ticks, panel_rows, rank), f32),
            pltpu.VMEM((ticks, chips, share, rank), f32),
            pltpu.VMEM((ticks, chips, share, rank), f32),
            pltpu.VMEM((groups, wide, rank), f32),
            pltpu.VMEM((chips, share, rank), f32),
            pltpu.VMEM((users, rank), f32),
            pltpu.VMEM((users, rank), bf16),
            pltpu.VMEM((users, rank), bf16),
            pltpu.VMEM((groups, users, wide), bf16),
            pltpu.VMEM((groups, users, wide), bf16),
            pltpu.VMEM((groups, wide, rank), bf16),
            pltpu.VMEM((groups, wide, rank), bf16),
            pltpu.VMEM((ticks, share, rank), f32),
        ] + [sems] * 8 + [pltpu.SemaphoreType.DMA((ticks,))] * 2 + [
            pltpu.VMEM(ratings.shape, ratings.dtype), pltpu.SemaphoreType.DMA((2,))],
        compiler_params=pltpu.CompilerParams(
            collective_id=0, has_side_effects=True, vmem_limit_bytes=48 * 1024 * 1024),
        cost_estimate=pl.CostEstimate(flops=work, bytes_accessed=8 * 1024 * 1024, transcendentals=0),
    )(slot_of, live, user_factors, item_factors, ratings)


def solution(mesh):
    both = ("band", "owner")
    placed = (P(both, None), P(both, None), P(None, both, None, None), P(None, both), P(None, both), P(None, both))
    return jax.shard_map(
        functools.partial(shards, mesh.shape["band"], mesh.shape["owner"]),
        mesh=mesh,
        in_specs=placed,
        out_specs=(P(both, None), P(both, None)),
        check_vma=False,
    )
```
